32 devices in a mesh: freq: 8 (over y, x, core), blk: 4 (over z).
Axes of the slice: x: 2, y: 2, z: 4, core: 2. Of those that a mesh axis runs over, the one named last changes fastest.
Arguments:
- traces: bfloat16 [32, 4096, 1024], P(('blk', 'freq')), may hold values from -6 to 6
- fir: float32 [128], replicated, may hold values from -0.5 to 0.5
- targets: int32 [256], replicated, may hold values from 0 to 31
- band: int32 [2], replicated, may hold values from 1 to 512, as said below
Outputs:
- multiples: float32 [32, 2, 256, 4096], P('freq', None, None, 'blk')
The draws below stay inside these ranges and needn't reach their ends.
Inputs may be any that keep to these rules, and one draw needn't show every extreme that they name: band[1] is 512 and band[1] - band[0] is at least 256.
All inputs are finite; a program needn't handle non-finite values.
Results may differ from the reference program's by a relative error of at most 0.019.
Values may be sent and summed in bfloat16 or wider, within the bound.
A program may use at most 128 MiB of HBM per device.

```python
import math
import jax
import jax.numpy as jnp
from jax import lax

NR = 4096
NT = 1024
TAPS = 128
TARGETS = 256
NS = 32
NF = 32
STRIDE = 128


def draw_band(key, part):
    band_high = jnp.asarray(NT // 2, jnp.int32)
    band_low = jax.random.randint(key, (), 1, NT // 4 + 1)
    return jnp.stack([band_low, band_high]).astype(jnp.int32)


def touch_ends(entries, rng, low, high):
    longest = entries.shape.index(max(entries.shape))
    spots = []
    for shift in (0, 1):
        where = [jax.random.randint(jax.random.fold_in(rng, axis), (), 0, length) for axis, length in enumerate(entries.shape)]
        where[longest] = (where[longest] + shift) % entries.shape[longest]
        spots.append(tuple(where))
    return entries.at[spots[0]].set(low).at[spots[1]].set(high)


def level_of(rng, dims, pieces, low, top_value):
    def one(axis_at, shards_of):
        steps = jax.random.uniform(jax.random.fold_in(jax.random.fold_in(rng, 6), axis_at), (shards_of,), jnp.float32, low / len(pieces), top_value / len(pieces))
        return jnp.repeat(jnp.exp(steps), dims[axis_at] // shards_of).reshape((-1,) + (1,) * (len(dims) - axis_at - 1))

    level = one(*pieces[0])
    for cut in pieces[1:]:
        level = level * one(*cut)
    return level


def centred(own_key, extent, deviation, reach, shards=(), kind=jnp.bfloat16):
    loudness = level_of(own_key, extent, shards, -0.22, 0.18) if shards else 1.0
    drawn = jax.random.normal(own_key, extent, jnp.float32) * deviation * loudness
    return jnp.minimum(jnp.maximum(drawn, -reach), reach).astype(kind)


def setup_inputs(seed: int = 0) -> dict:
    arg_keys = jax.random.split(jax.random.key(seed), 5)
    return {
        "traces": centred(arg_keys[0], (NS, NR, NT), 1.0, 6.0, ((0, 32),)),
        "fir": centred(arg_keys[1], (TAPS,), TAPS ** -0.5, 0.5, (), jnp.float32),
        "targets": touch_ends(jax.random.randint(arg_keys[2], (TARGETS,), 0, NS), jax.random.fold_in(arg_keys[2], 1), 0, NS - 1).astype(jnp.int32),
        "band": draw_band(jax.random.fold_in(arg_keys[4], 71), 0),
    }


def phase_table(band, freq_count, time_count):
    band_low = band[0]
    band_high = band[1]
    freq_index = jnp.arange(freq_count, dtype=jnp.int32)
    numerator = band_low * freq_count + (band_high - band_low) * freq_index
    time_index = jnp.arange(time_count, dtype=jnp.int32)
    turn_count = jnp.mod(time_index[:, None] * numerator[None, :], freq_count * time_count)
    phase_angle = turn_count.astype(jnp.float32) * (2.0 * math.pi / (freq_count * time_count))
    table = jnp.stack([jnp.cos(phase_angle), -jnp.sin(phase_angle)], axis=2) * (1.0 / math.sqrt(time_count))
    return table.reshape(time_count, 2 * freq_count)

def shaping_matrix(fir, time_count, tap_count):
    time_index = jnp.arange(time_count, dtype=jnp.int32)
    lag_table = time_index[None, :] - time_index[:, None]
    inside = (lag_table >= 0) & (lag_table < tap_count)
    values = fir[jnp.clip(lag_table, 0, tap_count - 1)]
    return jnp.where(inside, values, 0.0)

def reference(traces, fir, targets, band):
    dft_table = phase_table(band, NF, NT)
    mixed_table = jnp.dot(shaping_matrix(fir, NT, TAPS), dft_table, precision=lax.Precision.HIGHEST)

    def one_shot(shot_trace):
        out_rows = jnp.einsum('tc,rt->cr', mixed_table, shot_trace.astype(jnp.float32), precision=lax.Precision.HIGHEST)
        return out_rows.astype(jnp.bfloat16)
    spectrum = lax.map(one_shot, traces)
    spectrum = spectrum.reshape(NS, NF, 2, NR).transpose(1, 2, 0, 3)
    picked = jnp.take(spectrum, targets, axis=2)[..., ::STRIDE]
    chosen = jnp.swapaxes(picked, 2, 3)
    weight_scale = 1.0 / math.sqrt(NS)

    def one_freq(both_parts):
        target_rows, shot_rows = both_parts
        real_part = target_rows[0].astype(jnp.float32)
        imag_part = target_rows[1].astype(jnp.float32)
        left_block = jnp.stack([jnp.concatenate([real_part, -imag_part], 0), jnp.concatenate([imag_part, real_part], 0)])
        right_block = shot_rows.astype(jnp.float32).reshape(2 * NS, NR)
        return jnp.einsum('ojk,jr->okr', left_block, right_block, precision=lax.Precision.HIGHEST) * weight_scale
    return lax.map(one_freq, (chosen, spectrum))
```

```python
import functools
import math

import jax
import jax.numpy as jnp
from jax import lax
from jax.experimental import pallas as pl
from jax.experimental.pallas import tpu as pltpu
from jax.sharding import PartitionSpec as P

FREQ_DEV = 4
PARTS = 2 * FREQ_DEV
ROWS = 2 * PARTS
VMEM_LIMIT = 56 * 2**20
MESH = pl.DeviceIdType.MESH
NT_DIMS = (((1,), (1,)), ((), ()))


def dot(a, b, dims=(((1,), (0,)), ((), ())), precision=None):
    return lax.dot_general(a, b, dims, precision=precision, preferred_element_type=jnp.float32)


def cos_turns(turns):
    w = (0.25 - jnp.abs(turns - 0.5)) * (2.0 * math.pi)
    w2 = w * w
    total = jnp.full_like(w, 1.0 / math.factorial(13))
    for order in (11, 9, 7, 5, 3, 1):
        sign = 1.0 if order % 4 == 1 else -1.0
        total = total * w2 + sign / math.factorial(order)
    return -(total * w)


def send_kernel(
    freq_devs, blk_devs, col_stride,
    band_ref, fir_ref, traces_ref, recv_ref,
    traces_buf, spots_buf, table, outgoing, chunk_sem, spot_sem, own_sem, send_sem, recv_sem,
):
    me_f = lax.axis_index("freq")
    me_b = lax.axis_index("blk")
    me = me_b * freq_devs + me_f
    n = freq_devs * blk_devs
    spots, _, time_count = traces_buf.shape
    rec_count = spots * col_stride
    width = rec_count // blk_devs
    half = width // 2
    freq_count = FREQ_DEV * freq_devs
    cols = 2 * freq_count
    taps = fir_ref.shape[1]
    per = width // col_stride
    spot_lanes = outgoing.shape[3] - half

    def spot_copy():
        return pltpu.make_async_copy(
            traces_ref.at[:, pl.ds(0, 16), :], spots_buf, spot_sem
        )

    def chunk_copy(step):
        block = lax.rem(me_b + step + 1, blk_devs)
        return pltpu.make_async_copy(
            traces_ref.at[pl.ds(block * per, per)],
            traces_buf.at[pl.ds(step * per, per)],
            chunk_sem.at[step],
        )

    spot_copy().start()
    for step in range(blk_devs):
        chunk_copy(step).start()

    barrier = pltpu.get_barrier_semaphore()

    @pl.loop(1, n)
    def _(d):
        to = lax.rem(me + d, n)
        pl.semaphore_signal(
            barrier, inc=1, device_id=(lax.rem(to, freq_devs), to // freq_devs), device_id_type=MESH
        )

    row = lax.broadcasted_iota(jnp.int32, (cols, time_count), 0)
    time = lax.broadcasted_iota(jnp.int32, (cols, time_count), 1)
    period = freq_count * time_count
    low = band_ref[0]
    high = band_ref[1]
    numerator = low * freq_count + (high - low) * (row >> 1)
    turn = numerator * time

    def cosine(shift):
        return cos_turns(((turn + shift) & (period - 1)).astype(jnp.float32) * (1.0 / period))

    quarter = period // 4
    part = (row & 1) * quarter
    cos_full = cosine(part)
    sin_full = cosine(part + 3 * quarter)
    head = turn[:, :taps]
    lag = lax.broadcasted_iota(jnp.int32, (taps, taps), 0)
    late = lax.broadcasted_iota(jnp.int32, (taps, taps), 1)
    kept = jnp.where(lag < taps - late, 1.0, 0.0).astype(jnp.float32)
    fir = fir_ref[...]
    scale = 1.0 / math.sqrt(time_count)

    def head_cos(shift):
        return cos_turns(((head + shift) & (period - 1)).astype(jnp.float32) * (1.0 / period))

    sum_cos = dot(head_cos(0) * fir, kept, precision=lax.Precision.HIGHEST) * scale
    sum_sin = dot(head_cos(3 * quarter) * fir, kept, precision=lax.Precision.HIGHEST) * scale
    body = time_count - taps
    mixed = jnp.concatenate(
        [
            cos_full[:, :body] * sum_cos[:, :1] - sin_full[:, :body] * sum_sin[:, :1],
            cos_full[:, body:] * sum_cos - sin_full[:, body:] * sum_sin,
        ],
        1,
    )
    mixed_high = mixed.astype(jnp.bfloat16)
    table[pl.ds(0, cols), :] = mixed_high
    table[pl.ds(cols, cols), :] = (mixed - mixed_high.astype(jnp.float32)).astype(jnp.bfloat16)

    def spectrum_of(rows):
        both = dot(table[...], rows, NT_DIMS)
        return both[:cols] + both[cols:]

    spot_copy().wait()
    near = spectrum_of(spots_buf[...].reshape(spots * 16, time_count)).astype(jnp.bfloat16)
    spot_row = lax.broadcasted_iota(jnp.int32, (spots * 16, spot_lanes), 0)
    spot_col = lax.broadcasted_iota(jnp.int32, (spots * 16, spot_lanes), 1)
    pick = jnp.where(spot_row == spot_col * 16, 1.0, 0.0).astype(jnp.bfloat16)
    at_spots = dot(near, pick).reshape(freq_devs, PARTS, spot_lanes)
    at_spots = jnp.concatenate([at_spots, at_spots], 1).astype(jnp.bfloat16)
    pl.semaphore_wait(barrier, n - 1)

    def remote(step, f):
        block = lax.rem(me_b + step + 1, blk_devs)
        return pltpu.make_async_remote_copy(
            src_ref=outgoing.at[step, f],
            dst_ref=recv_ref.at[me],
            send_sem=send_sem.at[step * freq_devs + f],
            recv_sem=recv_sem.at[me],
            device_id=(f, block),
            device_id_type=MESH,
        )

    own = pltpu.make_async_copy(outgoing.at[blk_devs - 1, me_f], recv_ref.at[me], own_sem)
    for step in range(blk_devs):
        chunk_copy(step).wait()
        values = spectrum_of(
            traces_buf[pl.ds(step * per, per)].reshape(width, time_count)
        )
        values = values.reshape(freq_devs, PARTS, width)
        values = jnp.concatenate([values[:, :, :half], values[:, :, half:]], 1)
        outgoing[step, :, :, pl.ds(0, half)] = values.astype(jnp.bfloat16)
        outgoing[step, :, :, pl.ds(half, spot_lanes)] = at_spots
        first = 0
        if step == blk_devs - 1:
            own.start()
            first = 1

        @pl.loop(first, freq_devs)
        def _(d):
            remote(step, lax.rem(me_f + d, freq_devs)).start()

    own.wait()
    for step in range(blk_devs):

        @pl.loop(1 if step == blk_devs - 1 else 0, freq_devs)
        def _(d):
            remote(step, lax.rem(me_f + d, freq_devs)).wait_send()

    @pl.loop(1, n)
    def _(d):
        source = lax.rem(me + d, n)
        pltpu.make_async_remote_copy(
            src_ref=outgoing.at[0, 0],
            dst_ref=recv_ref.at[source],
            send_sem=send_sem.at[0],
            recv_sem=recv_sem.at[source],
            device_id=(lax.rem(source, freq_devs), source // freq_devs),
            device_id_type=MESH,
        ).wait_recv()


def product_kernel(targets_ref, recv_ref, out_ref):
    shots, rows, lanes = recv_ref.shape
    half = out_ref.shape[3] // 2
    spot_lanes = lanes - half
    depth = shots * rows
    count = targets_ref.shape[0]
    i = pl.program_id(0)
    received = recv_ref[...].reshape(depth, lanes)
    at_spots = received[:, half:]
    right = received[:, :half]
    column = lax.broadcasted_iota(jnp.int32, (count, depth), 1)
    base = targets_ref[...] * rows + 2 * i

    def chosen(part):
        return dot(jnp.where(column == base + part, 1.0, 0.0).astype(jnp.bfloat16), at_spots)

    real = chosen(0)
    imag = chosen(1)
    lefts = [
        jnp.concatenate([real, -imag], 1).astype(jnp.bfloat16),
        jnp.concatenate([imag, real], 1).astype(jnp.bfloat16),
    ]
    spot = lax.broadcasted_iota(jnp.int32, (2 * spot_lanes, depth), 0)
    place = lax.broadcasted_iota(jnp.int32, (2 * spot_lanes, depth), 1)
    home = jnp.where(spot < spot_lanes, spot * rows, (spot - spot_lanes) * rows + 1) + 2 * i
    scale = 1.0 / math.sqrt(shots)
    for h in range(2):
        spread = jnp.where(place == home + h * PARTS, 1.0, 0.0).astype(jnp.bfloat16)
        for o in range(2):
            left = dot(lefts[o], spread).astype(jnp.bfloat16)
            out_ref[0, o, :, pl.ds(h * half, half)] = dot(left, right) * scale


def per_device(traces, fir, targets, band):
    shot_dev, rec_count, time_count = traces.shape
    freq_devs = lax.axis_size("freq")
    blk_devs = lax.axis_size("blk")
    n = freq_devs * blk_devs
    assert shot_dev == 1
    col_stride = rec_count // n
    width = rec_count // blk_devs
    half = width // 2
    spot_lanes = max(128, n)
    lanes = half + spot_lanes
    cols = 2 * FREQ_DEV * freq_devs
    received = pl.pallas_call(
        functools.partial(send_kernel, freq_devs, blk_devs, col_stride),
        out_shape=jax.ShapeDtypeStruct((n, ROWS, lanes), jnp.bfloat16),
        in_specs=[
            pl.BlockSpec(memory_space=pltpu.SMEM),
            pl.BlockSpec(memory_space=pltpu.VMEM),
            pl.BlockSpec(memory_space=pl.ANY),
        ],
        out_specs=pl.BlockSpec(memory_space=pl.ANY),
        scratch_shapes=[
            pltpu.VMEM((n, col_stride, time_count), jnp.bfloat16),
            pltpu.VMEM((n, 16, time_count), jnp.bfloat16),
            pltpu.VMEM((2 * cols, time_count), jnp.bfloat16),
            pltpu.VMEM((blk_devs, freq_devs, ROWS, lanes), jnp.bfloat16),
            pltpu.SemaphoreType.DMA((blk_devs,)),
            pltpu.SemaphoreType.DMA,
            pltpu.SemaphoreType.DMA,
            pltpu.SemaphoreType.DMA((n,)),
            pltpu.SemaphoreType.DMA((n,)),
        ],
        compiler_params=pltpu.CompilerParams(
            collective_id=0, has_side_effects=True, vmem_limit_bytes=VMEM_LIMIT
        ),
    )(band, fir.reshape(1, -1), traces.reshape(n, col_stride, time_count))
    count = targets.shape[0]
    return pl.pallas_call(
        product_kernel,
        grid=(FREQ_DEV,),
        out_shape=jax.ShapeDtypeStruct((FREQ_DEV, 2, count, width), jnp.float32),
        in_specs=[
            pl.BlockSpec((count, 1), lambda i: (0, 0)),
            pl.BlockSpec((n, ROWS, lanes), lambda i: (0, 0, 0)),
        ],
        out_specs=pl.BlockSpec((1, 2, count, width), lambda i: (i, 0, 0, 0)),
        compiler_params=pltpu.CompilerParams(vmem_limit_bytes=VMEM_LIMIT),
    )(targets.reshape(-1, 1), received)


def solution(mesh):
    placed = (P(("blk", "freq"), None, None), P(), P(), P())
    return jax.shard_map(
        per_device,
        mesh=mesh,
        in_specs=placed,
        out_specs=P("freq", None, None, "blk"),
        check_vma=False,
    )
```

```python
import functools
import math

import jax
import jax.numpy as jnp
from jax import lax
from jax.experimental import pallas as pl
from jax.experimental.pallas import tpu as pltpu
from jax.sharding import PartitionSpec as P

FREQ_DEV = 4
PARTS = 2 * FREQ_DEV
ROWS = 2 * PARTS
VMEM_LIMIT = 56 * 2**20
MESH = pl.DeviceIdType.MESH
NT_DIMS = (((1,), (1,)), ((), ()))


def dot(a, b, dims=(((1,), (0,)), ((), ())), precision=None):
    return lax.dot_general(a, b, dims, precision=precision, preferred_element_type=jnp.float32)


def cos_turns(turns):
    w = (0.25 - jnp.abs(turns - 0.5)) * (2.0 * math.pi)
    w2 = w * w
    total = jnp.full_like(w, 1.0 / math.factorial(13))
    for order in (11, 9, 7, 5, 3, 1):
        sign = 1.0 if order % 4 == 1 else -1.0
        total = total * w2 + sign / math.factorial(order)
    return -(total * w)


def flipped(index, offset, count):
    total = 0
    bit = 1
    while bit < count:
        total = total + bit * lax.rem(index // bit + (offset // bit) % 2, 2)
        bit *= 2
    return total


def send_kernel(
    freq_devs, blk_devs, col_stride,
    band_ref, fir_ref, traces_ref, recv_ref,
    traces_buf, spots_buf, table, outgoing, chunk_sem, spot_sem, own_sem, send_sem, recv_sem,
):
    me_f = lax.axis_index("freq")
    me_b = lax.axis_index("blk")
    me = me_b * freq_devs + me_f
    n = freq_devs * blk_devs
    spots, _, time_count = traces_buf.shape
    rec_count = spots * col_stride
    width = rec_count // blk_devs
    half = width // 2
    freq_count = FREQ_DEV * freq_devs
    cols = 2 * freq_count
    taps = fir_ref.shape[1]
    per = width // col_stride
    spot_lanes = outgoing.shape[3] - half

    crossing = list(range(blk_devs // 2, blk_devs))
    offsets = crossing + list(range(blk_devs // 2 - 1, -1, -1))

    def spot_copy():
        return pltpu.make_async_copy(
            traces_ref.at[:, pl.ds(0, 16), :], spots_buf, spot_sem
        )

    def chunk_copy(step):
        block = flipped(me_b, offsets[step], blk_devs)
        return pltpu.make_async_copy(
            traces_ref.at[pl.ds(block * per, per)],
            traces_buf.at[pl.ds(step * per, per)],
            chunk_sem.at[step],
        )

    spot_copy().start()
    for step in range(blk_devs):
        chunk_copy(step).start()

    barrier = pltpu.get_barrier_semaphore()

    @pl.loop(1, n)
    def _(d):
        to = lax.rem(me + d, n)
        pl.semaphore_signal(
            barrier, inc=1, device_id=(lax.rem(to, freq_devs), to // freq_devs), device_id_type=MESH
        )

    row = lax.broadcasted_iota(jnp.int32, (cols, time_count), 0)
    time = lax.broadcasted_iota(jnp.int32, (cols, time_count), 1)
    period = freq_count * time_count
    low = band_ref[0]
    high = band_ref[1]
    numerator = low * freq_count + (high - low) * (row >> 1)
    turn = numerator * time

    def cosine(shift):
        return cos_turns(((turn + shift) & (period - 1)).astype(jnp.float32) * (1.0 / period))

    quarter = period // 4
    part = (row & 1) * quarter
    cos_full = cosine(part)
    sin_full = cosine(part + 3 * quarter)
    head = turn[:, :taps]
    lag = lax.broadcasted_iota(jnp.int32, (taps, taps), 0)
    late = lax.broadcasted_iota(jnp.int32, (taps, taps), 1)
    kept = jnp.where(lag < taps - late, 1.0, 0.0).astype(jnp.float32)
    fir = fir_ref[...]
    scale = 1.0 / math.sqrt(time_count)

    def head_cos(shift):
        return cos_turns(((head + shift) & (period - 1)).astype(jnp.float32) * (1.0 / period))

    sum_cos = dot(head_cos(0) * fir, kept, precision=lax.Precision.HIGHEST) * scale
    sum_sin = dot(head_cos(3 * quarter) * fir, kept, precision=lax.Precision.HIGHEST) * scale
    body = time_count - taps
    mixed = jnp.concatenate(
        [
            cos_full[:, :body] * sum_cos[:, :1] - sin_full[:, :body] * sum_sin[:, :1],
            cos_full[:, body:] * sum_cos - sin_full[:, body:] * sum_sin,
        ],
        1,
    )
    mixed_high = mixed.astype(jnp.bfloat16)
    table[pl.ds(0, cols), :] = mixed_high
    table[pl.ds(cols, cols), :] = (mixed - mixed_high.astype(jnp.float32)).astype(jnp.bfloat16)

    def spectrum_of(rows):
        both = dot(table[...], rows, NT_DIMS)
        return both[:cols] + both[cols:]

    spot_copy().wait()
    near = spectrum_of(spots_buf[...].reshape(spots * 16, time_count)).astype(jnp.bfloat16)
    spot_row = lax.broadcasted_iota(jnp.int32, (spots * 16, spot_lanes), 0)
    spot_col = lax.broadcasted_iota(jnp.int32, (spots * 16, spot_lanes), 1)
    spot_of = jnp.where(spot_col >= spots, spot_col - spots, spot_col)
    pick = jnp.where(spot_row == spot_of * 16, 1.0, 0.0).astype(jnp.bfloat16)
    at_spots = dot(near, pick).reshape(freq_devs, PARTS, spot_lanes)
    at_spots = jnp.concatenate([at_spots, at_spots], 1).astype(jnp.bfloat16)
    pl.semaphore_wait(barrier, n - 1)

    def remote(step, f):
        block = flipped(me_b, offsets[step], blk_devs)
        return pltpu.make_async_remote_copy(
            src_ref=outgoing.at[step, f],
            dst_ref=recv_ref.at[me],
            send_sem=send_sem.at[step * freq_devs + f],
            recv_sem=recv_sem.at[me],
            device_id=(f, block),
            device_id_type=MESH,
        )

    own = pltpu.make_async_copy(outgoing.at[blk_devs - 1, me_f], recv_ref.at[me], own_sem)
    for step in range(blk_devs):
        chunk_copy(step).wait()
        values = spectrum_of(
            traces_buf[pl.ds(step * per, per)].reshape(width, time_count)
        )
        values = values.reshape(freq_devs, PARTS, width)
        values = jnp.concatenate([values[:, :, :half], values[:, :, half:]], 1)
        outgoing[step, :, :, pl.ds(0, half)] = values.astype(jnp.bfloat16)
        outgoing[step, :, :, pl.ds(half, spot_lanes)] = at_spots
        first = 0
        if step == blk_devs - 1:
            own.start()
            first = 1

        @pl.loop(first, freq_devs)
        def _(d):
            remote(step, lax.rem(me_f + d, freq_devs)).start()

    own.wait()
    for step in range(blk_devs):

        @pl.loop(1 if step == blk_devs - 1 else 0, freq_devs)
        def _(d):
            remote(step, lax.rem(me_f + d, freq_devs)).wait_send()

    @pl.loop(1, n)
    def _(d):
        source = lax.rem(me + d, n)
        pltpu.make_async_remote_copy(
            src_ref=outgoing.at[0, 0],
            dst_ref=recv_ref.at[source],
            send_sem=send_sem.at[0],
            recv_sem=recv_sem.at[source],
            device_id=(lax.rem(source, freq_devs), source // freq_devs),
            device_id_type=MESH,
        ).wait_recv()


def product_kernel(targets_ref, recv_ref, out_ref):
    shots, rows, lanes = recv_ref.shape
    half = out_ref.shape[3] // 2
    depth = shots * rows
    spot_lanes = lanes - half
    count = targets_ref.shape[1]
    i = pl.program_id(0)

    line = lax.broadcasted_iota(jnp.int32, (4 * shots, depth), 0)
    place = lax.broadcasted_iota(jnp.int32, (4 * shots, depth), 1)
    group = line // shots
    home = (line - group * shots) * rows + (group // 2) * PARTS + (group & 1) + 2 * i
    pick = jnp.where(place == home, 1.0, 0.0).astype(jnp.bfloat16)
    picked = dot(pick, recv_ref[...].reshape(depth, lanes))

    wanted = jnp.broadcast_to(targets_ref[...].astype(jnp.float32), (128, count)).T
    shot = lax.broadcasted_iota(jnp.int32, (count, 2 * shots), 1)
    shot = jnp.where(shot >= shots, shot - shots, shot)
    chooser = jnp.where(shot == wanted[:, :1].astype(jnp.int32), 1.0, 0.0).astype(jnp.bfloat16)

    near = picked[: 2 * shots, half:]
    source = lax.broadcasted_iota(jnp.int32, near.shape, 0) >= shots
    lane = lax.broadcasted_iota(jnp.int32, near.shape, 1)
    target = lane >= shots
    inside = lane < 2 * shots
    same = inside & (source == target)
    other = inside & (source != target)
    parts = [
        jnp.where(same, jnp.where(source, -near, near), 0.0),
        jnp.where(other, near, 0.0),
    ]
    lefts = [dot(chooser, p.astype(jnp.bfloat16)).astype(jnp.bfloat16) for p in parts]
    scale = 1.0 / math.sqrt(shots)
    for h in range(2):
        right = picked[2 * shots * h : 2 * shots * (h + 1), :half].astype(jnp.bfloat16)
        for o in range(2):
            out_ref[0, o, :, pl.ds(h * half, half)] = dot(lefts[o][:, : 2 * shots], right) * scale


def per_device(traces, fir, targets, band):
    shot_dev, rec_count, time_count = traces.shape
    freq_devs = lax.axis_size("freq")
    blk_devs = lax.axis_size("blk")
    n = freq_devs * blk_devs
    assert shot_dev == 1
    assert blk_devs & (blk_devs - 1) == 0
    col_stride = rec_count // n
    width = rec_count // blk_devs
    half = width // 2
    spot_lanes = max(128, 2 * n)
    lanes = half + spot_lanes
    cols = 2 * FREQ_DEV * freq_devs
    received = pl.pallas_call(
        functools.partial(send_kernel, freq_devs, blk_devs, col_stride),
        out_shape=jax.ShapeDtypeStruct((n, ROWS, lanes), jnp.bfloat16),
        in_specs=[
            pl.BlockSpec(memory_space=pltpu.SMEM),
            pl.BlockSpec(memory_space=pltpu.VMEM),
            pl.BlockSpec(memory_space=pl.ANY),
        ],
        out_specs=pl.BlockSpec(memory_space=pl.ANY),
        scratch_shapes=[
            pltpu.VMEM((n, col_stride, time_count), jnp.bfloat16),
            pltpu.VMEM((n, 16, time_count), jnp.bfloat16),
            pltpu.VMEM((2 * cols, time_count), jnp.bfloat16),
            pltpu.VMEM((blk_devs, freq_devs, ROWS, lanes), jnp.bfloat16),
            pltpu.SemaphoreType.DMA((blk_devs,)),
            pltpu.SemaphoreType.DMA,
            pltpu.SemaphoreType.DMA,
            pltpu.SemaphoreType.DMA((n,)),
            pltpu.SemaphoreType.DMA((n,)),
        ],
        compiler_params=pltpu.CompilerParams(
            collective_id=0, has_side_effects=True, vmem_limit_bytes=VMEM_LIMIT
        ),
    )(band, fir.reshape(1, -1), traces.reshape(n, col_stride, time_count))
    count = targets.shape[0]
    return pl.pallas_call(
        product_kernel,
        grid=(FREQ_DEV,),
        out_shape=jax.ShapeDtypeStruct((FREQ_DEV, 2, count, width), jnp.float32),
        in_specs=[
            pl.BlockSpec((1, count), lambda i: (0, 0)),
            pl.BlockSpec((n, ROWS, lanes), lambda i: (0, 0, 0)),
        ],
        out_specs=pl.BlockSpec((1, 2, count, width), lambda i: (i, 0, 0, 0)),
        compiler_params=pltpu.CompilerParams(vmem_limit_bytes=VMEM_LIMIT),
    )(targets.reshape(1, -1), received)


def solution(mesh):
    placed = (P(("blk", "freq"), None, None), P(), P(), P())
    return jax.shard_map(
        per_device,
        mesh=mesh,
        in_specs=placed,
        out_specs=P("freq", None, None, "blk"),
        check_vma=False,
    )
```

```python
import functools
import math

import jax
import jax.numpy as jnp
from jax import lax
from jax.experimental import pallas as pl
from jax.experimental.pallas import tpu as pltpu
from jax.sharding import PartitionSpec as P

FREQ_DEV = 4
PARTS = 2 * FREQ_DEV
ROWS = 2 * PARTS
VMEM_LIMIT = 56 * 2**20
MESH = pl.DeviceIdType.MESH
NT_DIMS = (((1,), (1,)), ((), ()))


def dot(a, b, dims=(((1,), (0,)), ((), ())), precision=None):
    return lax.dot_general(a, b, dims, precision=precision, preferred_element_type=jnp.float32)


def cos_turns(turns):
    w = (0.25 - jnp.abs(turns - 0.5)) * (2.0 * math.pi)
    w2 = w * w
    total = jnp.full_like(w, 1.0 / math.factorial(13))
    for order in (11, 9, 7, 5, 3, 1):
        sign = 1.0 if order % 4 == 1 else -1.0
        total = total * w2 + sign / math.factorial(order)
    return -(total * w)


def flipped(index, offset, count):
    total = 0
    bit = 1
    while bit < count:
        total = total + bit * lax.rem(index // bit + (offset // bit) % 2, 2)
        bit *= 2
    return total


def send_kernel(
    freq_devs, blk_devs, col_stride,
    band_ref, fir_ref, traces_ref, recv_ref, plane_ref,
    traces_buf, spots_buf, table, outgoing, near_out, near_in, plane_out,
    chunk_sem, spot_sem, own_sem, send_sem, recv_sem,
    near_send, near_recv, plane_own, plane_send, plane_recv,
):
    me_f = lax.axis_index("freq")
    me_b = lax.axis_index("blk")
    me = me_b * freq_devs + me_f
    n = freq_devs * blk_devs
    spots, _, time_count = traces_buf.shape
    rec_count = spots * col_stride
    width = rec_count // blk_devs
    half = width // 2
    freq_count = FREQ_DEV * freq_devs
    cols = 2 * freq_count
    taps = fir_ref.shape[1]
    per = width // col_stride
    _, near_rows, near_lanes = near_out.shape
    packed = near_lanes // spots

    crossing = list(range(blk_devs // 2, blk_devs))
    offsets = crossing + list(range(blk_devs // 2 - 1, -1, -1))

    def spot_copy():
        return pltpu.make_async_copy(
            traces_ref.at[:, pl.ds(0, 16), :], spots_buf, spot_sem
        )

    def chunk_copy(step):
        block = flipped(me_b, offsets[step], blk_devs)
        return pltpu.make_async_copy(
            traces_ref.at[pl.ds(block * per, per)],
            traces_buf.at[pl.ds(step * per, per)],
            chunk_sem.at[step],
        )

    spot_copy().start()
    for step in range(blk_devs):
        chunk_copy(step).start()

    barrier = pltpu.get_barrier_semaphore()

    @pl.loop(1, n)
    def _(d):
        to = lax.rem(me + d, n)
        pl.semaphore_signal(
            barrier, inc=1, device_id=(lax.rem(to, freq_devs), to // freq_devs), device_id_type=MESH
        )

    row = lax.broadcasted_iota(jnp.int32, (cols, time_count), 0)
    time = lax.broadcasted_iota(jnp.int32, (cols, time_count), 1)
    period = freq_count * time_count
    low = band_ref[0]
    high = band_ref[1]
    numerator = low * freq_count + (high - low) * (row >> 1)
    turn = numerator * time

    def cosine(shift):
        return cos_turns(((turn + shift) & (period - 1)).astype(jnp.float32) * (1.0 / period))

    quarter = period // 4
    part = (row & 1) * quarter
    cos_full = cosine(part)
    sin_full = cosine(part + 3 * quarter)
    head = turn[:, :taps]
    lag = lax.broadcasted_iota(jnp.int32, (taps, taps), 0)
    late = lax.broadcasted_iota(jnp.int32, (taps, taps), 1)
    kept = jnp.where(lag < taps - late, 1.0, 0.0).astype(jnp.float32)
    fir = fir_ref[...]
    scale = 1.0 / math.sqrt(time_count)

    def head_cos(shift):
        return cos_turns(((head + shift) & (period - 1)).astype(jnp.float32) * (1.0 / period))

    sum_cos = dot(head_cos(0) * fir, kept, precision=lax.Precision.HIGHEST) * scale
    sum_sin = dot(head_cos(3 * quarter) * fir, kept, precision=lax.Precision.HIGHEST) * scale
    body = time_count - taps
    mixed = jnp.concatenate(
        [
            cos_full[:, :body] * sum_cos[:, :1] - sin_full[:, :body] * sum_sin[:, :1],
            cos_full[:, body:] * sum_cos - sin_full[:, body:] * sum_sin,
        ],
        1,
    )
    mixed_high = mixed.astype(jnp.bfloat16)
    table[pl.ds(0, cols), :] = mixed_high
    table[pl.ds(cols, cols), :] = (mixed - mixed_high.astype(jnp.float32)).astype(jnp.bfloat16)

    def spectrum_of(rows):
        both = dot(table[...], rows, NT_DIMS)
        return both[:cols] + both[cols:]

    spot_copy().wait()
    near = spectrum_of(spots_buf[...].reshape(spots * 16, time_count)).astype(jnp.bfloat16)
    spot_row = lax.broadcasted_iota(jnp.int32, (spots * 16, near_lanes), 0)
    spot_col = lax.broadcasted_iota(jnp.int32, (spots * 16, near_lanes), 1)
    shift = lax.rem(me_f, packed) * spots
    pick = jnp.where(spot_row == (spot_col - shift) * 16, 1.0, 0.0).astype(jnp.bfloat16)
    at_spots = dot(near, pick).reshape(freq_devs, PARTS, near_lanes)
    at_spots = jnp.concatenate([at_spots] * (near_rows // PARTS), 1)
    line = lax.broadcasted_iota(jnp.int32, at_spots.shape, 1) // PARTS
    near_out[...] = jnp.where(line == me_f // packed, at_spots, 0.0).astype(jnp.bfloat16)
    pl.semaphore_wait(barrier, n - 1)

    def near_copy(f, slot):
        return pltpu.make_async_remote_copy(
            src_ref=near_out.at[f],
            dst_ref=near_in.at[slot],
            send_sem=near_send.at[f],
            recv_sem=near_recv.at[slot],
            device_id=(f, me_b),
            device_id_type=MESH,
        )

    def plane_copy(offset, slot):
        return pltpu.make_async_remote_copy(
            src_ref=plane_out,
            dst_ref=plane_ref.at[slot],
            send_sem=plane_send.at[offset],
            recv_sem=plane_recv.at[slot],
            device_id=(me_f, flipped(me_b, offset, blk_devs)),
            device_id_type=MESH,
        )

    own_plane = pltpu.make_async_copy(plane_out, plane_ref.at[me_b], plane_own)

    @pl.loop(1, freq_devs)
    def _(d):
        near_copy(lax.rem(me_f + d, freq_devs), me_f).start()

    def remote(step, f):
        block = flipped(me_b, offsets[step], blk_devs)
        return pltpu.make_async_remote_copy(
            src_ref=outgoing.at[step, f],
            dst_ref=recv_ref.at[me],
            send_sem=send_sem.at[step * freq_devs + f],
            recv_sem=recv_sem.at[me],
            device_id=(f, block),
            device_id_type=MESH,
        )

    own = pltpu.make_async_copy(outgoing.at[blk_devs - 1, me_f], recv_ref.at[me], own_sem)
    for step in range(blk_devs):
        chunk_copy(step).wait()
        values = spectrum_of(
            traces_buf[pl.ds(step * per, per)].reshape(width, time_count)
        )
        values = values.reshape(freq_devs, PARTS, width)
        values = jnp.concatenate([values[:, :, :half], values[:, :, half:]], 1)
        outgoing[step] = values.astype(jnp.bfloat16)
        first = 0
        if step == blk_devs - 1:
            own.start()
            first = 1

        @pl.loop(first, freq_devs)
        def _(d):
            remote(step, lax.rem(me_f + d, freq_devs)).start()

        if step == blk_devs // 2 - 1:
            total = near_out[me_f].astype(jnp.float32)
            for d in range(1, freq_devs):
                source = lax.rem(me_f + d, freq_devs)
                near_copy(source, source).wait_recv()
                total = total + near_in[source].astype(jnp.float32)
            plane_out[...] = total.astype(jnp.bfloat16)
            own_plane.start()
            for offset in range(1, blk_devs):
                plane_copy(offset, me_b).start()

    own.wait()
    own_plane.wait()

    @pl.loop(1, freq_devs)
    def _(d):
        near_copy(lax.rem(me_f + d, freq_devs), me_f).wait_send()

    for offset in range(1, blk_devs):
        plane_copy(offset, me_b).wait_send()
        plane_copy(offset, flipped(me_b, offset, blk_devs)).wait_recv()
    for step in range(blk_devs):

        @pl.loop(1 if step == blk_devs - 1 else 0, freq_devs)
        def _(d):
            remote(step, lax.rem(me_f + d, freq_devs)).wait_send()

    @pl.loop(1, n)
    def _(d):
        source = lax.rem(me + d, n)
        pltpu.make_async_remote_copy(
            src_ref=outgoing.at[0, 0],
            dst_ref=recv_ref.at[source],
            send_sem=send_sem.at[0],
            recv_sem=recv_sem.at[source],
            device_id=(lax.rem(source, freq_devs), source // freq_devs),
            device_id_type=MESH,
        ).wait_recv()


def product_kernel(freq_devs, targets_ref, recv_ref, plane_ref, out_ref):
    shots, rows, lanes = recv_ref.shape
    blk_devs, near_rows, near_lanes = plane_ref.shape
    packed = near_lanes // shots
    half = out_ref.shape[3] // 2
    depth = shots * rows
    count = targets_ref.shape[1]
    i = pl.program_id(0)

    line = lax.broadcasted_iota(jnp.int32, (4 * shots, depth), 0)
    place = lax.broadcasted_iota(jnp.int32, (4 * shots, depth), 1)
    group = line // shots
    home = (line - group * shots) * rows + (group // 2) * PARTS + (group & 1) + 2 * i
    pick = jnp.where(place == home, 1.0, 0.0).astype(jnp.bfloat16)
    picked = dot(pick, recv_ref[...].reshape(depth, lanes))

    wanted = jnp.broadcast_to(targets_ref[...].astype(jnp.float32), (128, count)).T
    shot = lax.broadcasted_iota(jnp.int32, (count, 2 * shots), 1)
    shot = jnp.where(shot >= shots, shot - shots, shot)
    chooser = jnp.where(shot == wanted[:, :1].astype(jnp.int32), 1.0, 0.0).astype(jnp.bfloat16)

    near_depth = blk_devs * near_rows
    line = lax.broadcasted_iota(jnp.int32, (2 * shots, near_depth), 0)
    place = lax.broadcasted_iota(jnp.int32, (2 * shots, near_depth), 1)
    part = line // shots
    from_shot = line - part * shots
    from_f = from_shot % freq_devs
    home = (from_shot // freq_devs) * near_rows + (from_f // packed) * PARTS + 2 * i + part
    pick = jnp.where(place == home, 1.0, 0.0).astype(jnp.bfloat16)
    near = dot(pick, plane_ref[...].reshape(near_depth, near_lanes))
    slot = lax.broadcasted_iota(jnp.int32, near.shape, 0) % freq_devs % packed
    lane = lax.broadcasted_iota(jnp.int32, near.shape, 1)
    near = jnp.where(lane // shots == slot, near, 0.0).astype(jnp.bfloat16)
    fold_row = lax.broadcasted_iota(jnp.int32, (near_lanes, max(128, 2 * shots)), 0)
    fold_col = lax.broadcasted_iota(jnp.int32, (near_lanes, max(128, 2 * shots)), 1)
    fold = jnp.where(fold_row % shots == fold_col % shots, 1.0, 0.0).astype(jnp.bfloat16)
    near = dot(near, fold)
    source = lax.broadcasted_iota(jnp.int32, near.shape, 0) >= shots
    lane = lax.broadcasted_iota(jnp.int32, near.shape, 1)
    target = lane >= shots
    inside = lane < 2 * shots
    same = inside & (source == target)
    other = inside & (source != target)
    parts = [
        jnp.where(same, jnp.where(source, -near, near), 0.0),
        jnp.where(other, near, 0.0),
    ]
    lefts = [dot(chooser, p.astype(jnp.bfloat16)).astype(jnp.bfloat16) for p in parts]
    scale = 1.0 / math.sqrt(shots)
    for h in range(2):
        right = picked[2 * shots * h : 2 * shots * (h + 1), :half].astype(jnp.bfloat16)
        for o in range(2):
            out_ref[0, o, :, pl.ds(h * half, half)] = dot(lefts[o][:, : 2 * shots], right) * scale


def per_device(traces, fir, targets, band):
    shot_dev, rec_count, time_count = traces.shape
    freq_devs = lax.axis_size("freq")
    blk_devs = lax.axis_size("blk")
    n = freq_devs * blk_devs
    assert shot_dev == 1
    assert blk_devs & (blk_devs - 1) == 0
    col_stride = rec_count // n
    width = rec_count // blk_devs
    half = width // 2
    lanes = half
    near_lanes = max(128, n)
    packed = near_lanes // n
    near_rows = freq_devs // packed * PARTS
    cols = 2 * FREQ_DEV * freq_devs
    received, planes = pl.pallas_call(
        functools.partial(send_kernel, freq_devs, blk_devs, col_stride),
        out_shape=[
            jax.ShapeDtypeStruct((n, ROWS, lanes), jnp.bfloat16),
            jax.ShapeDtypeStruct((blk_devs, near_rows, near_lanes), jnp.bfloat16),
        ],
        in_specs=[
            pl.BlockSpec(memory_space=pltpu.SMEM),
            pl.BlockSpec(memory_space=pltpu.VMEM),
            pl.BlockSpec(memory_space=pl.ANY),
        ],
        out_specs=[pl.BlockSpec(memory_space=pl.ANY)] * 2,
        scratch_shapes=[
            pltpu.VMEM((n, col_stride, time_count), jnp.bfloat16),
            pltpu.VMEM((n, 16, time_count), jnp.bfloat16),
            pltpu.VMEM((2 * cols, time_count), jnp.bfloat16),
            pltpu.VMEM((blk_devs, freq_devs, ROWS, lanes), jnp.bfloat16),
            pltpu.VMEM((freq_devs, near_rows, near_lanes), jnp.bfloat16),
            pltpu.VMEM((freq_devs, near_rows, near_lanes), jnp.bfloat16),
            pltpu.VMEM((near_rows, near_lanes), jnp.bfloat16),
            pltpu.SemaphoreType.DMA((blk_devs,)),
            pltpu.SemaphoreType.DMA,
            pltpu.SemaphoreType.DMA,
            pltpu.SemaphoreType.DMA((n,)),
            pltpu.SemaphoreType.DMA((n,)),
            pltpu.SemaphoreType.DMA((freq_devs,)),
            pltpu.SemaphoreType.DMA((freq_devs,)),
            pltpu.SemaphoreType.DMA,
            pltpu.SemaphoreType.DMA((blk_devs,)),
            pltpu.SemaphoreType.DMA((blk_devs,)),
        ],
        compiler_params=pltpu.CompilerParams(
            collective_id=0, has_side_effects=True, vmem_limit_bytes=VMEM_LIMIT
        ),
    )(band, fir.reshape(1, -1), traces.reshape(n, col_stride, time_count))
    count = targets.shape[0]
    return pl.pallas_call(
        functools.partial(product_kernel, freq_devs),
        grid=(FREQ_DEV,),
        out_shape=jax.ShapeDtypeStruct((FREQ_DEV, 2, count, width), jnp.float32),
        in_specs=[
            pl.BlockSpec((1, count), lambda i: (0, 0)),
            pl.BlockSpec((n, ROWS, lanes), lambda i: (0, 0, 0)),
            pl.BlockSpec((blk_devs, near_rows, near_lanes), lambda i: (0, 0, 0)),
        ],
        out_specs=pl.BlockSpec((1, 2, count, width), lambda i: (i, 0, 0, 0)),
        compiler_params=pltpu.CompilerParams(vmem_limit_bytes=VMEM_LIMIT),
    )(targets.reshape(1, -1), received, planes)


def solution(mesh):
    placed = (P(("blk", "freq"), None, None), P(), P(), P())
    return jax.shard_map(
        per_device,
        mesh=mesh,
        in_specs=placed,
        out_specs=P("freq", None, None, "blk"),
        check_vma=False,
    )
```

```python
import functools
import math

import jax
import jax.numpy as jnp
from jax import lax
from jax.experimental import pallas as pl
from jax.experimental.pallas import tpu as pltpu
from jax.sharding import PartitionSpec as P

FREQ_DEV = 4
PARTS = 2 * FREQ_DEV
ROWS = 2 * PARTS
VMEM_LIMIT = 56 * 2**20
MESH = pl.DeviceIdType.MESH
NT_DIMS = (((1,), (1,)), ((), ()))


def dot(a, b, dims=(((1,), (0,)), ((), ())), precision=None):
    return lax.dot_general(a, b, dims, precision=precision, preferred_element_type=jnp.float32)


def cos_turns(turns):
    w = (0.25 - jnp.abs(turns - 0.5)) * (2.0 * math.pi)
    w2 = w * w
    total = jnp.full_like(w, 1.0 / math.factorial(13))
    for order in (11, 9, 7, 5, 3, 1):
        sign = 1.0 if order % 4 == 1 else -1.0
        total = total * w2 + sign / math.factorial(order)
    return -(total * w)


def flipped(index, offset, count):
    total = 0
    bit = 1
    while bit < count:
        total = total + bit * lax.rem(index // bit + (offset // bit) % 2, 2)
        bit *= 2
    return total


def send_kernel(
    freq_devs, blk_devs, col_stride,
    band_ref, fir_ref, traces_ref, recv_ref, plane_ref,
    traces_buf, spots_buf, table, outgoing, near_out, near_in, plane_out,
    chunk_sem, spot_sem, own_sem, send_sem, recv_sem,
    near_send, near_recv, plane_own, plane_send, plane_recv,
):
    me_f = lax.axis_index("freq")
    me_b = lax.axis_index("blk")
    me = me_b * freq_devs + me_f
    n = freq_devs * blk_devs
    spots, _, time_count = traces_buf.shape
    rec_count = spots * col_stride
    width = rec_count // blk_devs
    half = width // 2
    freq_count = FREQ_DEV * freq_devs
    cols = 2 * freq_count
    taps = fir_ref.shape[1]
    per = width // col_stride
    _, near_rows, near_lanes = near_out.shape
    packed = near_lanes // spots

    crossing = list(range(blk_devs // 2, blk_devs))
    offsets = crossing + list(range(blk_devs // 2 - 1, -1, -1))

    def spot_copy():
        return pltpu.make_async_copy(
            traces_ref.at[:, pl.ds(0, 16), :], spots_buf, spot_sem
        )

    def chunk_copy(step):
        block = flipped(me_b, offsets[step], blk_devs)
        return pltpu.make_async_copy(
            traces_ref.at[pl.ds(block * per, per)],
            traces_buf.at[pl.ds(step * per, per)],
            chunk_sem.at[step],
        )

    chunk_copy(0).start()
    spot_copy().start()
    for step in range(1, blk_devs):
        chunk_copy(step).start()

    barrier = pltpu.get_barrier_semaphore()

    @pl.loop(1, n)
    def _(d):
        to = lax.rem(me + d, n)
        pl.semaphore_signal(
            barrier, inc=1, device_id=(lax.rem(to, freq_devs), to // freq_devs), device_id_type=MESH
        )

    row = lax.broadcasted_iota(jnp.int32, (cols, time_count), 0)
    time = lax.broadcasted_iota(jnp.int32, (cols, time_count), 1)
    period = freq_count * time_count
    low = band_ref[0]
    high = band_ref[1]
    numerator = low * freq_count + (high - low) * (row >> 1)
    turn = numerator * time

    def cosine(shift):
        return cos_turns(((turn + shift) & (period - 1)).astype(jnp.float32) * (1.0 / period))

    quarter = period // 4
    part = (row & 1) * quarter
    cos_full = cosine(part)
    sin_full = cosine(part + 3 * quarter)
    head = turn[:, :taps]
    lag = lax.broadcasted_iota(jnp.int32, (taps, taps), 0)
    late = lax.broadcasted_iota(jnp.int32, (taps, taps), 1)
    kept = jnp.where(lag < taps - late, 1.0, 0.0).astype(jnp.float32)
    fir = fir_ref[...]
    scale = 1.0 / math.sqrt(time_count)

    def head_cos(shift):
        return cos_turns(((head + shift) & (period - 1)).astype(jnp.float32) * (1.0 / period))

    sum_cos = dot(head_cos(0) * fir, kept, precision=lax.Precision.HIGHEST) * scale
    sum_sin = dot(head_cos(3 * quarter) * fir, kept, precision=lax.Precision.HIGHEST) * scale
    body = time_count - taps
    mixed = jnp.concatenate(
        [
            cos_full[:, :body] * sum_cos[:, :1] - sin_full[:, :body] * sum_sin[:, :1],
            cos_full[:, body:] * sum_cos - sin_full[:, body:] * sum_sin,
        ],
        1,
    )
    mixed_high = mixed.astype(jnp.bfloat16)
    table[pl.ds(0, cols), :] = mixed_high
    table[pl.ds(cols, cols), :] = (mixed - mixed_high.astype(jnp.float32)).astype(jnp.bfloat16)

    def spectrum_of(rows):
        both = dot(table[...], rows, NT_DIMS)
        return both[:cols] + both[cols:]

    pl.semaphore_wait(barrier, n - 1)

    def near_copy(f, slot):
        return pltpu.make_async_remote_copy(
            src_ref=near_out.at[f],
            dst_ref=near_in.at[slot],
            send_sem=near_send.at[f],
            recv_sem=near_recv.at[slot],
            device_id=(f, me_b),
            device_id_type=MESH,
        )

    def plane_copy(offset, slot):
        return pltpu.make_async_remote_copy(
            src_ref=plane_out,
            dst_ref=plane_ref.at[slot],
            send_sem=plane_send.at[offset],
            recv_sem=plane_recv.at[slot],
            device_id=(me_f, flipped(me_b, offset, blk_devs)),
            device_id_type=MESH,
        )

    own_plane = pltpu.make_async_copy(plane_out, plane_ref.at[me_b], plane_own)

    def remote(step, f):
        block = flipped(me_b, offsets[step], blk_devs)
        return pltpu.make_async_remote_copy(
            src_ref=outgoing.at[step, f],
            dst_ref=recv_ref.at[me],
            send_sem=send_sem.at[step * freq_devs + f],
            recv_sem=recv_sem.at[me],
            device_id=(f, block),
            device_id_type=MESH,
        )

    own = pltpu.make_async_copy(outgoing.at[blk_devs - 1, me_f], recv_ref.at[me], own_sem)
    for step in range(blk_devs):
        chunk_copy(step).wait()
        values = spectrum_of(
            traces_buf[pl.ds(step * per, per)].reshape(width, time_count)
        )
        values = values.reshape(freq_devs, PARTS, width)
        values = jnp.concatenate([values[:, :, :half], values[:, :, half:]], 1)
        outgoing[step] = values.astype(jnp.bfloat16)
        first = 0
        if step == blk_devs - 1:
            own.start()
            first = 1

        @pl.loop(first, freq_devs)
        def _(d):
            remote(step, lax.rem(me_f + d, freq_devs)).start()

        if step == 0:
            spot_copy().wait()
            near = spectrum_of(spots_buf[...].reshape(spots * 16, time_count)).astype(jnp.bfloat16)
            spot_row = lax.broadcasted_iota(jnp.int32, (spots * 16, near_lanes), 0)
            spot_col = lax.broadcasted_iota(jnp.int32, (spots * 16, near_lanes), 1)
            shift = lax.rem(me_f, packed) * spots
            pick = jnp.where(spot_row == (spot_col - shift) * 16, 1.0, 0.0).astype(jnp.bfloat16)
            at_spots = dot(near, pick).reshape(freq_devs, PARTS, near_lanes)
            at_spots = jnp.concatenate([at_spots] * (near_rows // PARTS), 1)
            line = lax.broadcasted_iota(jnp.int32, at_spots.shape, 1) // PARTS
            near_out[...] = jnp.where(line == me_f // packed, at_spots, 0.0).astype(jnp.bfloat16)

            @pl.loop(1, freq_devs)
            def _(d):
                near_copy(lax.rem(me_f + d, freq_devs), me_f).start()

        if step == blk_devs - 2:
            total = near_out[me_f].astype(jnp.float32)
            for d in range(1, freq_devs):
                source = lax.rem(me_f + d, freq_devs)
                near_copy(source, source).wait_recv()
                total = total + near_in[source].astype(jnp.float32)
            plane_out[...] = total.astype(jnp.bfloat16)
            own_plane.start()
            for offset in range(1, blk_devs):
                plane_copy(offset, me_b).start()

    own.wait()
    own_plane.wait()

    @pl.loop(1, freq_devs)
    def _(d):
        near_copy(lax.rem(me_f + d, freq_devs), me_f).wait_send()

    for offset in range(1, blk_devs):
        plane_copy(offset, me_b).wait_send()
        plane_copy(offset, flipped(me_b, offset, blk_devs)).wait_recv()
    for step in range(blk_devs):

        @pl.loop(1 if step == blk_devs - 1 else 0, freq_devs)
        def _(d):
            remote(step, lax.rem(me_f + d, freq_devs)).wait_send()

    @pl.loop(1, n)
    def _(d):
        source = lax.rem(me + d, n)
        pltpu.make_async_remote_copy(
            src_ref=outgoing.at[0, 0],
            dst_ref=recv_ref.at[source],
            send_sem=send_sem.at[0],
            recv_sem=recv_sem.at[source],
            device_id=(lax.rem(source, freq_devs), source // freq_devs),
            device_id_type=MESH,
        ).wait_recv()


def product_kernel(freq_devs, targets_ref, recv_ref, plane_ref, out_ref, made, sems):
    shots, rows, lanes = recv_ref.shape
    blk_devs, near_rows, near_lanes = plane_ref.shape
    packed = near_lanes // shots
    half = made.shape[3] // 2
    depth = shots * rows
    count = targets_ref.shape[1]

    wanted = jnp.broadcast_to(targets_ref[...].astype(jnp.float32), (128, count)).T
    shot = lax.broadcasted_iota(jnp.int32, (count, 2 * shots), 1)
    shot = jnp.where(shot >= shots, shot - shots, shot)
    chooser = jnp.where(shot == wanted[:, :1].astype(jnp.int32), 1.0, 0.0).astype(jnp.bfloat16)
    fold_row = lax.broadcasted_iota(jnp.int32, (near_lanes, max(128, 2 * shots)), 0)
    fold_col = lax.broadcasted_iota(jnp.int32, (near_lanes, max(128, 2 * shots)), 1)
    fold = jnp.where(fold_row % shots == fold_col % shots, 1.0, 0.0).astype(jnp.bfloat16)
    scale = 1.0 / math.sqrt(shots)

    def write(i, o):
        return pltpu.make_async_copy(made.at[i, o], out_ref.at[i, o], sems.at[i, o])

    for i in range(FREQ_DEV):
        line = lax.broadcasted_iota(jnp.int32, (4 * shots, depth), 0)
        place = lax.broadcasted_iota(jnp.int32, (4 * shots, depth), 1)
        group = line // shots
        home = (line - group * shots) * rows + (group // 2) * PARTS + (group & 1) + 2 * i
        pick = jnp.where(place == home, 1.0, 0.0).astype(jnp.bfloat16)
        picked = dot(pick, recv_ref[...].reshape(depth, lanes))

        near_depth = blk_devs * near_rows
        line = lax.broadcasted_iota(jnp.int32, (2 * shots, near_depth), 0)
        place = lax.broadcasted_iota(jnp.int32, (2 * shots, near_depth), 1)
        part = line // shots
        from_shot = line - part * shots
        from_f = from_shot % freq_devs
        home = (from_shot // freq_devs) * near_rows + (from_f // packed) * PARTS + 2 * i + part
        pick = jnp.where(place == home, 1.0, 0.0).astype(jnp.bfloat16)
        near = dot(pick, plane_ref[...].reshape(near_depth, near_lanes))
        slot = lax.broadcasted_iota(jnp.int32, near.shape, 0) % freq_devs % packed
        lane = lax.broadcasted_iota(jnp.int32, near.shape, 1)
        near = jnp.where(lane // shots == slot, near, 0.0).astype(jnp.bfloat16)
        near = dot(near, fold)
        source = lax.broadcasted_iota(jnp.int32, near.shape, 0) >= shots
        lane = lax.broadcasted_iota(jnp.int32, near.shape, 1)
        target = lane >= shots
        inside = lane < 2 * shots
        same = inside & (source == target)
        other = inside & (source != target)
        parts = [
            jnp.where(same, jnp.where(source, -near, near), 0.0),
            jnp.where(other, near, 0.0),
        ]
        lefts = [dot(chooser, p.astype(jnp.bfloat16)).astype(jnp.bfloat16) for p in parts]
        rights = [
            picked[2 * shots * h : 2 * shots * (h + 1), :half].astype(jnp.bfloat16) for h in range(2)
        ]
        for o in range(2):
            for h in range(2):
                made[i, o, :, pl.ds(h * half, half)] = dot(lefts[o][:, : 2 * shots], rights[h]) * scale
            write(i, o).start()

    for i in range(FREQ_DEV):
        for o in range(2):
            write(i, o).wait()


def per_device(traces, fir, targets, band):
    shot_dev, rec_count, time_count = traces.shape
    freq_devs = lax.axis_size("freq")
    blk_devs = lax.axis_size("blk")
    n = freq_devs * blk_devs
    assert shot_dev == 1
    assert blk_devs & (blk_devs - 1) == 0
    col_stride = rec_count // n
    width = rec_count // blk_devs
    half = width // 2
    lanes = half
    near_lanes = max(128, n)
    packed = near_lanes // n
    near_rows = freq_devs // packed * PARTS
    cols = 2 * FREQ_DEV * freq_devs
    received, planes = pl.pallas_call(
        functools.partial(send_kernel, freq_devs, blk_devs, col_stride),
        out_shape=[
            jax.ShapeDtypeStruct((n, ROWS, lanes), jnp.bfloat16),
            jax.ShapeDtypeStruct((blk_devs, near_rows, near_lanes), jnp.bfloat16),
        ],
        in_specs=[
            pl.BlockSpec(memory_space=pltpu.SMEM),
            pl.BlockSpec(memory_space=pltpu.VMEM),
            pl.BlockSpec(memory_space=pl.ANY),
        ],
        out_specs=[pl.BlockSpec(memory_space=pl.ANY)] * 2,
        scratch_shapes=[
            pltpu.VMEM((n, col_stride, time_count), jnp.bfloat16),
            pltpu.VMEM((n, 16, time_count), jnp.bfloat16),
            pltpu.VMEM((2 * cols, time_count), jnp.bfloat16),
            pltpu.VMEM((blk_devs, freq_devs, ROWS, lanes), jnp.bfloat16),
            pltpu.VMEM((freq_devs, near_rows, near_lanes), jnp.bfloat16),
            pltpu.VMEM((freq_devs, near_rows, near_lanes), jnp.bfloat16),
            pltpu.VMEM((near_rows, near_lanes), jnp.bfloat16),
            pltpu.SemaphoreType.DMA((blk_devs,)),
            pltpu.SemaphoreType.DMA,
            pltpu.SemaphoreType.DMA,
            pltpu.SemaphoreType.DMA((n,)),
            pltpu.SemaphoreType.DMA((n,)),
            pltpu.SemaphoreType.DMA((freq_devs,)),
            pltpu.SemaphoreType.DMA((freq_devs,)),
            pltpu.SemaphoreType.DMA,
            pltpu.SemaphoreType.DMA((blk_devs,)),
            pltpu.SemaphoreType.DMA((blk_devs,)),
        ],
        compiler_params=pltpu.CompilerParams(
            collective_id=0, has_side_effects=True, vmem_limit_bytes=VMEM_LIMIT
        ),
    )(band, fir.reshape(1, -1), traces.reshape(n, col_stride, time_count))
    count = targets.shape[0]
    return pl.pallas_call(
        functools.partial(product_kernel, freq_devs),
        out_shape=jax.ShapeDtypeStruct((FREQ_DEV, 2, count, width), jnp.float32),
        in_specs=[pl.BlockSpec(memory_space=pltpu.VMEM)] * 3,
        out_specs=pl.BlockSpec(memory_space=pl.ANY),
        scratch_shapes=[
            pltpu.VMEM((FREQ_DEV, 2, count, width), jnp.float32),
            pltpu.SemaphoreType.DMA((FREQ_DEV, 2)),
        ],
        compiler_params=pltpu.CompilerParams(vmem_limit_bytes=VMEM_LIMIT),
    )(targets.reshape(1, -1), received, planes)


def solution(mesh):
    placed = (P(("blk", "freq"), None, None), P(), P(), P())
    return jax.shard_map(
        per_device,
        mesh=mesh,
        in_specs=placed,
        out_specs=P("freq", None, None, "blk"),
        check_vma=False,
    )
```

```python
import functools
import math

import jax
import jax.numpy as jnp
from jax import lax
from jax.experimental import pallas as pl
from jax.experimental.pallas import tpu as pltpu
from jax.sharding import PartitionSpec as P

FREQ_DEV = 4
PARTS = 2 * FREQ_DEV
ROWS = 2 * PARTS
VMEM_LIMIT = 56 * 2**20
MESH = pl.DeviceIdType.MESH
NT_DIMS = (((1,), (1,)), ((), ()))


def dot(a, b, dims=(((1,), (0,)), ((), ())), precision=None):
    return lax.dot_general(a, b, dims, precision=precision, preferred_element_type=jnp.float32)


def cos_turns(turns):
    w = (0.25 - jnp.abs(turns - 0.5)) * (2.0 * math.pi)
    w2 = w * w
    total = jnp.full_like(w, 1.0 / math.factorial(13))
    for order in (11, 9, 7, 5, 3, 1):
        sign = 1.0 if order % 4 == 1 else -1.0
        total = total * w2 + sign / math.factorial(order)
    return -(total * w)


def flipped(index, offset, count):
    total = 0
    bit = 1
    while bit < count:
        total = total + bit * lax.rem(index // bit + (offset // bit) % 2, 2)
        bit *= 2
    return total


def send_kernel(
    freq_devs, blk_devs, col_stride,
    band_ref, fir_ref, traces_ref, recv_ref, plane_ref,
    traces_buf, spots_buf, table, outgoing, near_out, near_in, plane_out,
    chunk_sem, spot_sem, own_sem, send_sem, recv_sem,
    near_send, near_recv, plane_own, plane_send, plane_recv,
):
    me_f = lax.axis_index("freq")
    me_b = lax.axis_index("blk")
    me = me_b * freq_devs + me_f
    n = freq_devs * blk_devs
    spots, _, time_count = traces_buf.shape
    rec_count = spots * col_stride
    width = rec_count // blk_devs
    half = width // 2
    freq_count = FREQ_DEV * freq_devs
    cols = 2 * freq_count
    taps = fir_ref.shape[1]
    per = width // col_stride
    _, near_rows, near_lanes = near_out.shape
    packed = near_lanes // spots

    crossing = list(range(blk_devs // 2, blk_devs))
    offsets = crossing + list(range(blk_devs // 2 - 1, -1, -1))

    def spot_copy():
        return pltpu.make_async_copy(
            traces_ref.at[:, pl.ds(0, 16), :], spots_buf, spot_sem
        )

    def chunk_copy(step):
        block = flipped(me_b, offsets[step], blk_devs)
        return pltpu.make_async_copy(
            traces_ref.at[pl.ds(block * per, per)],
            traces_buf.at[pl.ds(step * per, per)],
            chunk_sem.at[step],
        )

    chunk_copy(0).start()
    spot_copy().start()
    for step in range(1, blk_devs):
        chunk_copy(step).start()

    barrier = pltpu.get_barrier_semaphore()

    @pl.loop(1, n)
    def _(d):
        to = lax.rem(me + d, n)
        pl.semaphore_signal(
            barrier, inc=1, device_id=(lax.rem(to, freq_devs), to // freq_devs), device_id_type=MESH
        )

    row = lax.broadcasted_iota(jnp.int32, (cols, time_count), 0)
    time = lax.broadcasted_iota(jnp.int32, (cols, time_count), 1)
    period = freq_count * time_count
    low = band_ref[0]
    high = band_ref[1]
    numerator = low * freq_count + (high - low) * (row >> 1)
    turn = numerator * time

    def cosine(shift):
        return cos_turns(((turn + shift) & (period - 1)).astype(jnp.float32) * (1.0 / period))

    quarter = period // 4
    part = (row & 1) * quarter
    cos_full = cosine(part)
    sin_full = cosine(part + 3 * quarter)
    head = turn[:, :taps]
    lag = lax.broadcasted_iota(jnp.int32, (taps, taps), 0)
    late = lax.broadcasted_iota(jnp.int32, (taps, taps), 1)
    kept = jnp.where(lag < taps - late, 1.0, 0.0).astype(jnp.float32)
    fir = fir_ref[...]
    scale = 1.0 / math.sqrt(time_count)

    def head_cos(shift):
        return cos_turns(((head + shift) & (period - 1)).astype(jnp.float32) * (1.0 / period))

    sum_cos = dot(head_cos(0) * fir, kept, precision=lax.Precision.HIGHEST) * scale
    sum_sin = dot(head_cos(3 * quarter) * fir, kept, precision=lax.Precision.HIGHEST) * scale
    body = time_count - taps
    mixed = jnp.concatenate(
        [
            cos_full[:, :body] * sum_cos[:, :1] - sin_full[:, :body] * sum_sin[:, :1],
            cos_full[:, body:] * sum_cos - sin_full[:, body:] * sum_sin,
        ],
        1,
    )
    mixed_high = mixed.astype(jnp.bfloat16)
    table[pl.ds(0, cols), :] = mixed_high
    table[pl.ds(cols, cols), :] = (mixed - mixed_high.astype(jnp.float32)).astype(jnp.bfloat16)

    def spectrum_of(rows):
        both = dot(table[...], rows, NT_DIMS)
        return both[:cols] + both[cols:]


    def near_copy(f, slot):
        return pltpu.make_async_remote_copy(
            src_ref=near_out.at[f],
            dst_ref=near_in.at[slot],
            send_sem=near_send.at[f],
            recv_sem=near_recv.at[slot],
            device_id=(f, me_b),
            device_id_type=MESH,
        )

    def plane_copy(offset, slot):
        return pltpu.make_async_remote_copy(
            src_ref=plane_out,
            dst_ref=plane_ref.at[slot],
            send_sem=plane_send.at[offset],
            recv_sem=plane_recv.at[slot],
            device_id=(me_f, flipped(me_b, offset, blk_devs)),
            device_id_type=MESH,
        )

    own_plane = pltpu.make_async_copy(plane_out, plane_ref.at[me_b], plane_own)

    def remote(step, f):
        block = flipped(me_b, offsets[step], blk_devs)
        return pltpu.make_async_remote_copy(
            src_ref=outgoing.at[step, f],
            dst_ref=recv_ref.at[me],
            send_sem=send_sem.at[step * freq_devs + f],
            recv_sem=recv_sem.at[me],
            device_id=(f, block),
            device_id_type=MESH,
        )

    own = pltpu.make_async_copy(outgoing.at[blk_devs - 1, me_f], recv_ref.at[me], own_sem)
    for step in range(blk_devs):
        chunk_copy(step).wait()
        values = spectrum_of(
            traces_buf[pl.ds(step * per, per)].reshape(width, time_count)
        )
        values = values.reshape(freq_devs, PARTS, width)
        values = jnp.concatenate([values[:, :, :half], values[:, :, half:]], 1)
        outgoing[step] = values.astype(jnp.bfloat16)
        if step == 0:
            pl.semaphore_wait(barrier, n - 1)
        first = 0
        if step == blk_devs - 1:
            own.start()
            first = 1

        @pl.loop(first, freq_devs)
        def _(d):
            remote(step, lax.rem(me_f + d, freq_devs)).start()

        if step == 0:
            spot_copy().wait()
            near = spectrum_of(spots_buf[...].reshape(spots * 16, time_count)).astype(jnp.bfloat16)
            spot_row = lax.broadcasted_iota(jnp.int32, (spots * 16, near_lanes), 0)
            spot_col = lax.broadcasted_iota(jnp.int32, (spots * 16, near_lanes), 1)
            shift = lax.rem(me_f, packed) * spots
            pick = jnp.where(spot_row == (spot_col - shift) * 16, 1.0, 0.0).astype(jnp.bfloat16)
            at_spots = dot(near, pick).reshape(freq_devs, PARTS, near_lanes)
            at_spots = jnp.concatenate([at_spots] * (near_rows // PARTS), 1)
            line = lax.broadcasted_iota(jnp.int32, at_spots.shape, 1) // PARTS
            near_out[...] = jnp.where(line == me_f // packed, at_spots, 0.0).astype(jnp.bfloat16)

            @pl.loop(1, freq_devs)
            def _(d):
                near_copy(lax.rem(me_f + d, freq_devs), me_f).start()

        if step == blk_devs - 2:
            total = near_out[me_f].astype(jnp.float32)
            for d in range(1, freq_devs):
                source = lax.rem(me_f + d, freq_devs)
                near_copy(source, source).wait_recv()
                total = total + near_in[source].astype(jnp.float32)
            plane_out[...] = total.astype(jnp.bfloat16)
            own_plane.start()
            for offset in range(1, blk_devs):
                plane_copy(offset, me_b).start()

    own.wait()
    own_plane.wait()

    @pl.loop(1, freq_devs)
    def _(d):
        near_copy(lax.rem(me_f + d, freq_devs), me_f).wait_send()

    for offset in range(1, blk_devs):
        plane_copy(offset, me_b).wait_send()
        plane_copy(offset, flipped(me_b, offset, blk_devs)).wait_recv()
    for step in range(blk_devs):

        @pl.loop(1 if step == blk_devs - 1 else 0, freq_devs)
        def _(d):
            remote(step, lax.rem(me_f + d, freq_devs)).wait_send()

    @pl.loop(1, n)
    def _(d):
        source = lax.rem(me + d, n)
        pltpu.make_async_remote_copy(
            src_ref=outgoing.at[0, 0],
            dst_ref=recv_ref.at[source],
            send_sem=send_sem.at[0],
            recv_sem=recv_sem.at[source],
            device_id=(lax.rem(source, freq_devs), source // freq_devs),
            device_id_type=MESH,
        ).wait_recv()


def product_kernel(freq_devs, targets_ref, recv_ref, plane_ref, out_ref, made, sems):
    shots, rows, lanes = recv_ref.shape
    blk_devs, near_rows, near_lanes = plane_ref.shape
    packed = near_lanes // shots
    half = made.shape[3] // 2
    depth = shots * rows
    count = targets_ref.shape[1]

    wanted = jnp.broadcast_to(targets_ref[...].astype(jnp.float32), (128, count)).T
    shot = lax.broadcasted_iota(jnp.int32, (count, 2 * shots), 1)
    shot = jnp.where(shot >= shots, shot - shots, shot)
    chooser = jnp.where(shot == wanted[:, :1].astype(jnp.int32), 1.0, 0.0).astype(jnp.bfloat16)
    fold_row = lax.broadcasted_iota(jnp.int32, (near_lanes, max(128, 2 * shots)), 0)
    fold_col = lax.broadcasted_iota(jnp.int32, (near_lanes, max(128, 2 * shots)), 1)
    fold = jnp.where(fold_row % shots == fold_col % shots, 1.0, 0.0).astype(jnp.bfloat16)
    scale = 1.0 / math.sqrt(shots)

    def write(i, o):
        return pltpu.make_async_copy(made.at[i, o], out_ref.at[i, o], sems.at[i, o])

    for i in range(FREQ_DEV):
        line = lax.broadcasted_iota(jnp.int32, (4 * shots, depth), 0)
        place = lax.broadcasted_iota(jnp.int32, (4 * shots, depth), 1)
        group = line // shots
        home = (line - group * shots) * rows + (group // 2) * PARTS + (group & 1) + 2 * i
        pick = jnp.where(place == home, 1.0, 0.0).astype(jnp.bfloat16)
        picked = dot(pick, recv_ref[...].reshape(depth, lanes))

        near_depth = blk_devs * near_rows
        line = lax.broadcasted_iota(jnp.int32, (2 * shots, near_depth), 0)
        place = lax.broadcasted_iota(jnp.int32, (2 * shots, near_depth), 1)
        part = line // shots
        from_shot = line - part * shots
        from_f = from_shot % freq_devs
        home = (from_shot // freq_devs) * near_rows + (from_f // packed) * PARTS + 2 * i + part
        pick = jnp.where(place == home, 1.0, 0.0).astype(jnp.bfloat16)
        near = dot(pick, plane_ref[...].reshape(near_depth, near_lanes))
        slot = lax.broadcasted_iota(jnp.int32, near.shape, 0) % freq_devs % packed
        lane = lax.broadcasted_iota(jnp.int32, near.shape, 1)
        near = jnp.where(lane // shots == slot, near, 0.0).astype(jnp.bfloat16)
        near = dot(near, fold)
        source = lax.broadcasted_iota(jnp.int32, near.shape, 0) >= shots
        lane = lax.broadcasted_iota(jnp.int32, near.shape, 1)
        target = lane >= shots
        inside = lane < 2 * shots
        same = inside & (source == target)
        other = inside & (source != target)
        parts = [
            jnp.where(same, jnp.where(source, -near, near), 0.0),
            jnp.where(other, near, 0.0),
        ]
        lefts = [dot(chooser, p.astype(jnp.bfloat16)).astype(jnp.bfloat16) for p in parts]
        rights = [
            picked[2 * shots * h : 2 * shots * (h + 1), :half].astype(jnp.bfloat16) for h in range(2)
        ]
        for o in range(2):
            for h in range(2):
                made[i, o, :, pl.ds(h * half, half)] = dot(lefts[o][:, : 2 * shots], rights[h]) * scale
            write(i, o).start()

    for i in range(FREQ_DEV):
        for o in range(2):
            write(i, o).wait()


def per_device(traces, fir, targets, band):
    shot_dev, rec_count, time_count = traces.shape
    freq_devs = lax.axis_size("freq")
    blk_devs = lax.axis_size("blk")
    n = freq_devs * blk_devs
    assert shot_dev == 1
    assert blk_devs & (blk_devs - 1) == 0
    col_stride = rec_count // n
    width = rec_count // blk_devs
    half = width // 2
    lanes = half
    near_lanes = max(128, n)
    packed = near_lanes // n
    near_rows = freq_devs // packed * PARTS
    cols = 2 * FREQ_DEV * freq_devs
    received, planes = pl.pallas_call(
        functools.partial(send_kernel, freq_devs, blk_devs, col_stride),
        out_shape=[
            jax.ShapeDtypeStruct((n, ROWS, lanes), jnp.bfloat16),
            jax.ShapeDtypeStruct((blk_devs, near_rows, near_lanes), jnp.bfloat16),
        ],
        in_specs=[
            pl.BlockSpec(memory_space=pltpu.SMEM),
            pl.BlockSpec(memory_space=pltpu.VMEM),
            pl.BlockSpec(memory_space=pl.ANY),
        ],
        out_specs=[pl.BlockSpec(memory_space=pl.ANY)] * 2,
        scratch_shapes=[
            pltpu.VMEM((n, col_stride, time_count), jnp.bfloat16),
            pltpu.VMEM((n, 16, time_count), jnp.bfloat16),
            pltpu.VMEM((2 * cols, time_count), jnp.bfloat16),
            pltpu.VMEM((blk_devs, freq_devs, ROWS, lanes), jnp.bfloat16),
            pltpu.VMEM((freq_devs, near_rows, near_lanes), jnp.bfloat16),
            pltpu.VMEM((freq_devs, near_rows, near_lanes), jnp.bfloat16),
            pltpu.VMEM((near_rows, near_lanes), jnp.bfloat16),
            pltpu.SemaphoreType.DMA((blk_devs,)),
            pltpu.SemaphoreType.DMA,
            pltpu.SemaphoreType.DMA,
            pltpu.SemaphoreType.DMA((n,)),
            pltpu.SemaphoreType.DMA((n,)),
            pltpu.SemaphoreType.DMA((freq_devs,)),
            pltpu.SemaphoreType.DMA((freq_devs,)),
            pltpu.SemaphoreType.DMA,
            pltpu.SemaphoreType.DMA((blk_devs,)),
            pltpu.SemaphoreType.DMA((blk_devs,)),
        ],
        compiler_params=pltpu.CompilerParams(
            collective_id=0, has_side_effects=True, vmem_limit_bytes=VMEM_LIMIT
        ),
    )(band, fir.reshape(1, -1), traces.reshape(n, col_stride, time_count))
    count = targets.shape[0]
    return pl.pallas_call(
        functools.partial(product_kernel, freq_devs),
        out_shape=jax.ShapeDtypeStruct((FREQ_DEV, 2, count, width), jnp.float32),
        in_specs=[pl.BlockSpec(memory_space=pltpu.VMEM)] * 3,
        out_specs=pl.BlockSpec(memory_space=pl.ANY),
        scratch_shapes=[
            pltpu.VMEM((FREQ_DEV, 2, count, width), jnp.float32),
            pltpu.SemaphoreType.DMA((FREQ_DEV, 2)),
        ],
        compiler_params=pltpu.CompilerParams(vmem_limit_bytes=VMEM_LIMIT),
    )(targets.reshape(1, -1), received, planes)


def solution(mesh):
    placed = (P(("blk", "freq"), None, None), P(), P(), P())
    return jax.shard_map(
        per_device,
        mesh=mesh,
        in_specs=placed,
        out_specs=P("freq", None, None, "blk"),
        check_vma=False,
    )
```

```python
import functools
import math

import jax
import jax.numpy as jnp
from jax import lax
from jax.experimental import pallas as pl
from jax.experimental.pallas import tpu as pltpu
from jax.sharding import PartitionSpec as P

FREQ_DEV = 4
PARTS = 2 * FREQ_DEV
ROWS = 2 * PARTS
VMEM_LIMIT = 56 * 2**20
MESH = pl.DeviceIdType.MESH


def dot(a, b, dims=(((1,), (0,)), ((), ())), precision=None):
    return lax.dot_general(a, b, dims, precision=precision, preferred_element_type=jnp.float32)


def cos_turns(turns):
    w = (0.25 - jnp.abs(turns - 0.5)) * (2.0 * math.pi)
    w2 = w * w
    total = jnp.full_like(w, 1.0 / math.factorial(13))
    for order in (11, 9, 7, 5, 3, 1):
        sign = 1.0 if order % 4 == 1 else -1.0
        total = total * w2 + sign / math.factorial(order)
    return -(total * w)


def flipped(index, offset, count):
    total = 0
    bit = 1
    while bit < count:
        total = total + bit * lax.rem(index // bit + (offset // bit) % 2, 2)
        bit *= 2
    return total


def send_kernel(
    freq_devs, blk_devs, col_stride,
    band_ref, fir_ref, traces_ref, recv_ref, plane_ref,
    traces_buf, spots_buf, table, outgoing, near_out, near_in, plane_out,
    chunk_sem, spot_sem, own_sem, send_sem, recv_sem,
    near_send, near_recv, plane_own, plane_send, plane_recv,
):
    me_f = lax.axis_index("freq")
    me_b = lax.axis_index("blk")
    me = me_b * freq_devs + me_f
    n = freq_devs * blk_devs
    spots, _, time_count = traces_buf.shape
    rec_count = spots * col_stride
    width = rec_count // blk_devs
    half = width // 2
    freq_count = FREQ_DEV * freq_devs
    cols = 2 * freq_count
    taps = fir_ref.shape[1]
    per = width // col_stride
    _, near_rows, near_lanes = near_out.shape
    packed = near_lanes // spots

    crossing = list(range(blk_devs // 2, blk_devs))
    offsets = crossing + list(range(blk_devs // 2 - 1, -1, -1))

    def spot_copy():
        return pltpu.make_async_copy(
            traces_ref.at[:, pl.ds(0, 16), :], spots_buf, spot_sem
        )

    def chunk_copy(step):
        block = flipped(me_b, offsets[step], blk_devs)
        return pltpu.make_async_copy(
            traces_ref.at[pl.ds(block * per, per)],
            traces_buf.at[pl.ds(step * per, per)],
            chunk_sem.at[step],
        )

    chunk_copy(0).start()
    spot_copy().start()
    for step in range(1, blk_devs):
        chunk_copy(step).start()

    barrier = pltpu.get_barrier_semaphore()

    @pl.loop(1, n)
    def _(d):
        to = lax.rem(me + d, n)
        pl.semaphore_signal(
            barrier, inc=1, device_id=(lax.rem(to, freq_devs), to // freq_devs), device_id_type=MESH
        )

    row = lax.broadcasted_iota(jnp.int32, (cols, time_count), 0)
    time = lax.broadcasted_iota(jnp.int32, (cols, time_count), 1)
    period = freq_count * time_count
    low = band_ref[0]
    high = band_ref[1]
    numerator = low * freq_count + (high - low) * (row >> 1)
    turn = numerator * time

    def cosine(shift):
        return cos_turns(((turn + shift) & (period - 1)).astype(jnp.float32) * (1.0 / period))

    quarter = period // 4
    part = (row & 1) * quarter
    cos_full = cosine(part)
    sin_full = cosine(part + 3 * quarter)
    head = turn[:, :taps]
    lag = lax.broadcasted_iota(jnp.int32, (taps, taps), 0)
    late = lax.broadcasted_iota(jnp.int32, (taps, taps), 1)
    kept = jnp.where(lag < taps - late, 1.0, 0.0).astype(jnp.float32)
    fir = fir_ref[...]
    scale = 1.0 / math.sqrt(time_count)

    def head_cos(shift):
        return cos_turns(((head + shift) & (period - 1)).astype(jnp.float32) * (1.0 / period))

    sum_cos = dot(head_cos(0) * fir, kept, precision=lax.Precision.HIGHEST) * scale
    sum_sin = dot(head_cos(3 * quarter) * fir, kept, precision=lax.Precision.HIGHEST) * scale
    body = time_count - taps
    mixed = jnp.concatenate(
        [
            cos_full[:, :body] * sum_cos[:, :1] - sin_full[:, :body] * sum_sin[:, :1],
            cos_full[:, body:] * sum_cos - sin_full[:, body:] * sum_sin,
        ],
        1,
    )
    mixed_high = mixed.astype(jnp.bfloat16)
    mixed_low = mixed - mixed_high.astype(jnp.float32)
    table[...] = (
        jnp.concatenate([mixed_high.astype(jnp.float32), mixed_low], 0).T.astype(jnp.bfloat16)
    )

    def spectrum_of(rows):
        both = dot(rows, table[...]).T
        return both[:cols] + both[cols:]


    def near_copy(f, slot):
        return pltpu.make_async_remote_copy(
            src_ref=near_out.at[f],
            dst_ref=near_in.at[slot],
            send_sem=near_send.at[f],
            recv_sem=near_recv.at[slot],
            device_id=(f, me_b),
            device_id_type=MESH,
        )

    def plane_copy(offset, slot):
        return pltpu.make_async_remote_copy(
            src_ref=plane_out,
            dst_ref=plane_ref.at[slot],
            send_sem=plane_send.at[offset],
            recv_sem=plane_recv.at[slot],
            device_id=(me_f, flipped(me_b, offset, blk_devs)),
            device_id_type=MESH,
        )

    own_plane = pltpu.make_async_copy(plane_out, plane_ref.at[me_b], plane_own)

    def remote(step, f):
        block = flipped(me_b, offsets[step], blk_devs)
        return pltpu.make_async_remote_copy(
            src_ref=outgoing.at[step, f],
            dst_ref=recv_ref.at[me],
            send_sem=send_sem.at[step * freq_devs + f],
            recv_sem=recv_sem.at[me],
            device_id=(f, block),
            device_id_type=MESH,
        )

    own = pltpu.make_async_copy(outgoing.at[blk_devs - 1, me_f], recv_ref.at[me], own_sem)
    for step in range(blk_devs):
        chunk_copy(step).wait()
        values = spectrum_of(
            traces_buf[pl.ds(step * per, per)].reshape(width, time_count)
        )
        values = values.reshape(freq_devs, PARTS, width)
        values = jnp.concatenate([values[:, :, :half], values[:, :, half:]], 1)
        outgoing[step] = values.astype(jnp.bfloat16)
        if step == 0:
            pl.semaphore_wait(barrier, n - 1)
        first = 0
        if step == blk_devs - 1:
            own.start()
            first = 1

        @pl.loop(first, freq_devs)
        def _(d):
            remote(step, lax.rem(me_f + d, freq_devs)).start()

        if step == 0:
            spot_copy().wait()
            near = spectrum_of(spots_buf[...].reshape(spots * 16, time_count)).astype(jnp.bfloat16)
            spot_row = lax.broadcasted_iota(jnp.int32, (spots * 16, near_lanes), 0)
            spot_col = lax.broadcasted_iota(jnp.int32, (spots * 16, near_lanes), 1)
            shift = lax.rem(me_f, packed) * spots
            pick = jnp.where(spot_row == (spot_col - shift) * 16, 1.0, 0.0).astype(jnp.bfloat16)
            at_spots = dot(near, pick).reshape(freq_devs, PARTS, near_lanes)
            at_spots = jnp.concatenate([at_spots] * (near_rows // PARTS), 1)
            line = lax.broadcasted_iota(jnp.int32, at_spots.shape, 1) // PARTS
            near_out[...] = jnp.where(line == me_f // packed, at_spots, 0.0).astype(jnp.bfloat16)

            @pl.loop(1, freq_devs)
            def _(d):
                near_copy(lax.rem(me_f + d, freq_devs), me_f).start()

        if step == blk_devs - 2:
            total = near_out[me_f].astype(jnp.float32)
            for d in range(1, freq_devs):
                source = lax.rem(me_f + d, freq_devs)
                near_copy(source, source).wait_recv()
                total = total + near_in[source].astype(jnp.float32)
            plane_out[...] = total.astype(jnp.bfloat16)
            own_plane.start()
            for offset in range(1, blk_devs):
                plane_copy(offset, me_b).start()

    own.wait()
    own_plane.wait()

    @pl.loop(1, freq_devs)
    def _(d):
        near_copy(lax.rem(me_f + d, freq_devs), me_f).wait_send()

    for offset in range(1, blk_devs):
        plane_copy(offset, me_b).wait_send()
        plane_copy(offset, flipped(me_b, offset, blk_devs)).wait_recv()
    for step in range(blk_devs):

        @pl.loop(1 if step == blk_devs - 1 else 0, freq_devs)
        def _(d):
            remote(step, lax.rem(me_f + d, freq_devs)).wait_send()

    @pl.loop(1, n)
    def _(d):
        source = lax.rem(me + d, n)
        pltpu.make_async_remote_copy(
            src_ref=outgoing.at[0, 0],
            dst_ref=recv_ref.at[source],
            send_sem=send_sem.at[0],
            recv_sem=recv_sem.at[source],
            device_id=(lax.rem(source, freq_devs), source // freq_devs),
            device_id_type=MESH,
        ).wait_recv()


def product_kernel(freq_devs, targets_ref, recv_ref, plane_ref, out_ref, made, sems):
    shots, rows, lanes = recv_ref.shape
    blk_devs, near_rows, near_lanes = plane_ref.shape
    packed = near_lanes // shots
    half = made.shape[3] // 2
    depth = shots * rows
    count = targets_ref.shape[1]

    wanted = jnp.broadcast_to(targets_ref[...].astype(jnp.float32), (128, count)).T
    shot = lax.broadcasted_iota(jnp.int32, (count, 2 * shots), 1)
    shot = jnp.where(shot >= shots, shot - shots, shot)
    chooser = jnp.where(shot == wanted[:, :1].astype(jnp.int32), 1.0, 0.0).astype(jnp.bfloat16)
    fold_row = lax.broadcasted_iota(jnp.int32, (near_lanes, max(128, 2 * shots)), 0)
    fold_col = lax.broadcasted_iota(jnp.int32, (near_lanes, max(128, 2 * shots)), 1)
    fold = jnp.where(fold_row % shots == fold_col % shots, 1.0, 0.0).astype(jnp.bfloat16)
    scale = 1.0 / math.sqrt(shots)

    def write(i, o):
        return pltpu.make_async_copy(made.at[i, o], out_ref.at[i, o], sems.at[i, o])

    for i in range(FREQ_DEV):
        line = lax.broadcasted_iota(jnp.int32, (4 * shots, depth), 0)
        place = lax.broadcasted_iota(jnp.int32, (4 * shots, depth), 1)
        group = line // shots
        home = (line - group * shots) * rows + (group // 2) * PARTS + (group & 1) + 2 * i
        pick = jnp.where(place == home, 1.0, 0.0).astype(jnp.bfloat16)
        picked = dot(pick, recv_ref[...].reshape(depth, lanes))

        near_depth = blk_devs * near_rows
        line = lax.broadcasted_iota(jnp.int32, (2 * shots, near_depth), 0)
        place = lax.broadcasted_iota(jnp.int32, (2 * shots, near_depth), 1)
        part = line // shots
        from_shot = line - part * shots
        from_f = from_shot % freq_devs
        home = (from_shot // freq_devs) * near_rows + (from_f // packed) * PARTS + 2 * i + part
        pick = jnp.where(place == home, 1.0, 0.0).astype(jnp.bfloat16)
        near = dot(pick, plane_ref[...].reshape(near_depth, near_lanes))
        slot = lax.broadcasted_iota(jnp.int32, near.shape, 0) % freq_devs % packed
        lane = lax.broadcasted_iota(jnp.int32, near.shape, 1)
        near = jnp.where(lane // shots == slot, near, 0.0).astype(jnp.bfloat16)
        near = dot(near, fold)
        source = lax.broadcasted_iota(jnp.int32, near.shape, 0) >= shots
        lane = lax.broadcasted_iota(jnp.int32, near.shape, 1)
        target = lane >= shots
        inside = lane < 2 * shots
        same = inside & (source == target)
        other = inside & (source != target)
        parts = [
            jnp.where(same, jnp.where(source, -near, near), 0.0),
            jnp.where(other, near, 0.0),
        ]
        lefts = [dot(chooser, p.astype(jnp.bfloat16)).astype(jnp.bfloat16) for p in parts]
        rights = [
            picked[2 * shots * h : 2 * shots * (h + 1), :half].astype(jnp.bfloat16) for h in range(2)
        ]
        for o in range(2):
            for h in range(2):
                made[i, o, :, pl.ds(h * half, half)] = dot(lefts[o][:, : 2 * shots], rights[h]) * scale
            write(i, o).start()

    for i in range(FREQ_DEV):
        for o in range(2):
            write(i, o).wait()


def per_device(traces, fir, targets, band):
    shot_dev, rec_count, time_count = traces.shape
    freq_devs = lax.axis_size("freq")
    blk_devs = lax.axis_size("blk")
    n = freq_devs * blk_devs
    assert shot_dev == 1
    assert blk_devs & (blk_devs - 1) == 0
    col_stride = rec_count // n
    width = rec_count // blk_devs
    half = width // 2
    lanes = half
    near_lanes = max(128, n)
    packed = near_lanes // n
    near_rows = freq_devs // packed * PARTS
    cols = 2 * FREQ_DEV * freq_devs
    received, planes = pl.pallas_call(
        functools.partial(send_kernel, freq_devs, blk_devs, col_stride),
        out_shape=[
            jax.ShapeDtypeStruct((n, ROWS, lanes), jnp.bfloat16),
            jax.ShapeDtypeStruct((blk_devs, near_rows, near_lanes), jnp.bfloat16),
        ],
        in_specs=[
            pl.BlockSpec(memory_space=pltpu.SMEM),
            pl.BlockSpec(memory_space=pltpu.VMEM),
            pl.BlockSpec(memory_space=pl.ANY),
        ],
        out_specs=[pl.BlockSpec(memory_space=pl.ANY)] * 2,
        scratch_shapes=[
            pltpu.VMEM((n, col_stride, time_count), jnp.bfloat16),
            pltpu.VMEM((n, 16, time_count), jnp.bfloat16),
            pltpu.VMEM((time_count, 2 * cols), jnp.bfloat16),
            pltpu.VMEM((blk_devs, freq_devs, ROWS, lanes), jnp.bfloat16),
            pltpu.VMEM((freq_devs, near_rows, near_lanes), jnp.bfloat16),
            pltpu.VMEM((freq_devs, near_rows, near_lanes), jnp.bfloat16),
            pltpu.VMEM((near_rows, near_lanes), jnp.bfloat16),
            pltpu.SemaphoreType.DMA((blk_devs,)),
            pltpu.SemaphoreType.DMA,
            pltpu.SemaphoreType.DMA,
            pltpu.SemaphoreType.DMA((n,)),
            pltpu.SemaphoreType.DMA((n,)),
            pltpu.SemaphoreType.DMA((freq_devs,)),
            pltpu.SemaphoreType.DMA((freq_devs,)),
            pltpu.SemaphoreType.DMA,
            pltpu.SemaphoreType.DMA((blk_devs,)),
            pltpu.SemaphoreType.DMA((blk_devs,)),
        ],
        compiler_params=pltpu.CompilerParams(
            collective_id=0, has_side_effects=True, vmem_limit_bytes=VMEM_LIMIT
        ),
    )(band, fir.reshape(1, -1), traces.reshape(n, col_stride, time_count))
    count = targets.shape[0]
    return pl.pallas_call(
        functools.partial(product_kernel, freq_devs),
        out_shape=jax.ShapeDtypeStruct((FREQ_DEV, 2, count, width), jnp.float32),
        in_specs=[pl.BlockSpec(memory_space=pltpu.VMEM)] * 3,
        out_specs=pl.BlockSpec(memory_space=pl.ANY),
        scratch_shapes=[
            pltpu.VMEM((FREQ_DEV, 2, count, width), jnp.float32),
            pltpu.SemaphoreType.DMA((FREQ_DEV, 2)),
        ],
        compiler_params=pltpu.CompilerParams(vmem_limit_bytes=VMEM_LIMIT),
    )(targets.reshape(1, -1), received, planes)


def solution(mesh):
    placed = (P(("blk", "freq"), None, None), P(), P(), P())
    return jax.shard_map(
        per_device,
        mesh=mesh,
        in_specs=placed,
        out_specs=P("freq", None, None, "blk"),
        check_vma=False,
    )
```
